32 devices in a mesh: tok: 16 (over z, y, x), head: 2 (over core).
Axes of the slice: x: 2, y: 2, z: 4, core: 2. Of those that a mesh axis runs over, the one named last changes fastest.
Arguments:
- queries: bfloat16 [2, 12288, 1536], P(None, 'tok', 'head'), may hold values from -16 to 16
- key_rows: bfloat16 [2, 12288, 1536], P(None, 'tok', 'head'), may hold values from -8 to 8
- value_rows: bfloat16 [2, 12288, 1536], P(None, 'tok', 'head'), may hold values from -6 to 6
- step_rates: float32 [4, 2, 12288], P('head', None, 'tok'), may hold values from 0.01 to 1
- gate_init: float32 [4, 384, 384], P('head'), may hold values from -0.3125 to 0.3125
- up_init: float32 [4, 384, 384], P('head'), may hold values from -0.3125 to 0.3125
- down_init: float32 [4, 384, 384], P('head'), may hold values from -0.3125 to 0.3125
- out_weight: bfloat16 [1536, 1536], P('head'), may hold values from -0.15625 to 0.15625
Outputs:
- mixed_out: bfloat16 [2, 12288, 1536], P(None, 'tok', 'head')
The draws below stay inside these ranges and needn't reach their ends.
All inputs are finite; a program needn't handle non-finite values.
Results may differ from the reference program's by a relative error of at most 0.009.
Values may be sent and summed in bfloat16 or wider, within the bound.
A program may use at most 128 MiB of HBM per device.

```python
import math
import jax
import jax.numpy as jnp
from jax import lax

D = 1536
HEADS = 4
DH = 384
FH = 384
WINDOW = 384
BLOCKS = 2
BLOCK = 12288


def draw_pair(base_key):
    shape = (BLOCKS, BLOCK, HEADS * DH)
    keyed = jax.random.fold_in(base_key, 7177)
    first_key, second_key = jax.random.split(keyed, 2)
    query_draw = jnp.clip(jax.random.normal(first_key, shape, jnp.float32), -8.0, 8.0)
    key_draw = jnp.clip(jax.random.normal(second_key, shape, jnp.float32), -8.0, 8.0)
    return (query_draw, key_draw)


def draw_queries(key, part):
    return draw_pair(key)[0].astype(jnp.bfloat16)


def draw_key_rows(key, part):
    return draw_pair(key)[1].astype(jnp.bfloat16)


def draw_step_rates(key, part):
    shape = (HEADS, BLOCKS, BLOCK)
    keyed = jax.random.fold_in(key, 9311)
    unit = jax.random.uniform(keyed, shape, jnp.float32)
    position = jnp.arange(BLOCK).astype(jnp.float32) / (BLOCK - 1)
    ramp = jnp.exp(jnp.log(0.15) * (1.0 - position))
    factor = jnp.exp(jnp.log(0.1) * (1.0 - unit))
    return (factor * ramp[None, None, :]).astype(jnp.float32)


def block_scale(own_key, shape, pieces, low, top_value):
    gain = 1.0
    for dim, blocks in pieces:
        heights = jax.random.uniform(jax.random.fold_in(jax.random.fold_in(own_key, 6), dim), (blocks,), jnp.float32, low / len(pieces), top_value / len(pieces))
        gain = gain * jnp.repeat(jnp.exp(heights), shape[dim] // blocks).reshape((-1,) + (1,) * (len(shape) - 1 - dim))
    return gain


def centred(rng, dims, deviation, most, cuts=(), kind=jnp.bfloat16):
    drawn = jax.random.normal(rng, dims, jnp.float32) * deviation
    if len(cuts) > 0:
        drawn = block_scale(rng, dims, cuts, -0.22, 0.18) * drawn
    return jnp.clip(drawn, min=-most, max=most).astype(kind)


def setup_inputs(seed: int = 0) -> dict:
    key_list = jax.random.split(jax.random.key(seed), 9)
    queries = draw_queries(jax.random.fold_in(key_list[8], 71), 0)
    key_rows = draw_key_rows(jax.random.fold_in(key_list[8], 71), 0)
    value_rows = centred(key_list[2], (BLOCKS, BLOCK, HEADS * DH), 1.0, 6.0, ((1, 16), (2, 2)))
    step_rates = draw_step_rates(jax.random.fold_in(key_list[8], 71), 0)
    gate_init = centred(key_list[4], (HEADS, FH, DH), DH ** -0.5, 0.3125, ((0, 2),), jnp.float32)
    up_init = centred(key_list[5], (HEADS, FH, DH), DH ** -0.5, 0.3125, ((0, 2),), jnp.float32)
    down_init = centred(key_list[6], (HEADS, DH, FH), FH ** -0.5, 0.3125, ((0, 2),), jnp.float32)
    out_weight = centred(key_list[7], (HEADS * DH, D), (HEADS * DH) ** -0.5, 0.15625, ((0, 2),))
    return {"queries": queries, "key_rows": key_rows, "value_rows": value_rows, "step_rates": step_rates, "gate_init": gate_init, "up_init": up_init, "down_init": down_init, "out_weight": out_weight}


EPSILON = 1e-06

def silu_slope(values_in):
    sigmoid_at = jax.nn.sigmoid(values_in)
    return sigmoid_at * (1.0 + values_in * (1.0 - sigmoid_at))

def row_scale(matrix):
    return jnp.sqrt(lax.optimization_barrier(jnp.mean(matrix * matrix, axis=-1, keepdims=True)) + EPSILON)

def renormed(old_weight, gradient, rate_sum):
    updated = old_weight - gradient / rate_sum
    return updated * (row_scale(old_weight) / row_scale(updated))

def window_attention(queries, key_rows, value_rows):
    length = queries.shape[0] * queries.shape[1]
    flat_queries = queries.reshape(length, HEADS, DH)
    zero_rows = jnp.zeros((WINDOW, HEADS, DH), jnp.bfloat16)
    flat_keys = jnp.concatenate([zero_rows, key_rows.reshape(length, HEADS, DH)], axis=0)
    flat_values = jnp.concatenate([zero_rows, value_rows.reshape(length, HEADS, DH)], axis=0)
    score_scale = 1.0 / math.sqrt(DH)

    def one_block(block_index):
        first_row = (block_index * WINDOW).astype(jnp.int32)
        query_block = lax.dynamic_slice_in_dim(flat_queries, first_row, WINDOW, 0).astype(jnp.float32)
        key_block = lax.dynamic_slice_in_dim(flat_keys, first_row, 2 * WINDOW, 0).astype(jnp.float32)
        value_block = lax.dynamic_slice_in_dim(flat_values, first_row, 2 * WINDOW, 0).astype(jnp.float32)
        scores = jnp.einsum('qhd,khd->hqk', query_block, key_block) * score_scale
        offset = jnp.arange(2 * WINDOW)[None, :] - WINDOW - jnp.arange(WINDOW)[:, None]
        global_key = first_row + jnp.arange(2 * WINDOW) - WINDOW
        allowed = (offset <= 0) & (offset > -WINDOW) & (global_key >= 0)[None, :]
        scores = jnp.where(allowed[None], scores, -jnp.inf)
        row_max = lax.optimization_barrier(jnp.max(scores, axis=-1, keepdims=True))
        expos = jnp.exp(scores - row_max)
        weights_bf = (expos / lax.optimization_barrier(jnp.sum(expos, axis=-1, keepdims=True))).astype(jnp.bfloat16)
        return jnp.einsum('hqk,khd->qhd', weights_bf.astype(jnp.float32), value_block)
    results = lax.map(one_block, jnp.arange(length // WINDOW, dtype=jnp.int32))
    return results.reshape(queries.shape[0], queries.shape[1], HEADS, DH)

def reference(queries, key_rows, value_rows, step_rates, gate_init, up_init, down_init, out_weight):
    attention = window_attention(queries, key_rows, value_rows)
    gate_now, up_now, down_now = (gate_init, up_init, down_init)
    outputs = []
    for block_at in range(BLOCKS):
        head_list = []
        gate_list, up_list, down_list = ([], [], [])
        for head_at in range(HEADS):
            lower = head_at * DH
            key_now = key_rows[block_at][:, lower:lower + DH]
            value_now = value_rows[block_at][:, lower:lower + DH]
            query_now = queries[block_at][:, lower:lower + DH]
            rate_now = step_rates[head_at, block_at]
            cast_gate = gate_now[head_at].astype(jnp.bfloat16)
            cast_up = up_now[head_at].astype(jnp.bfloat16)
            cast_down = down_now[head_at].astype(jnp.bfloat16)
            errors = (rate_now[:, None] * value_now.astype(jnp.float32)).astype(jnp.bfloat16)
            pre_gate = jnp.dot(key_now, cast_gate.T, preferred_element_type=jnp.float32)
            pre_up = jnp.dot(key_now, cast_up.T, preferred_element_type=jnp.float32)
            active = jax.nn.silu(pre_gate)
            hidden = (active * pre_up).astype(jnp.bfloat16)
            backed = jnp.dot(errors, cast_down, preferred_element_type=jnp.float32)
            back_up = (-backed * active).astype(jnp.bfloat16)
            back_gate = (-backed * pre_up * silu_slope(pre_gate)).astype(jnp.bfloat16)
            grad_gate = jnp.dot(back_gate.T, key_now, preferred_element_type=jnp.float32)
            grad_up = jnp.dot(back_up.T, key_now, preferred_element_type=jnp.float32)
            grad_down = -jnp.dot(errors.T, hidden, preferred_element_type=jnp.float32)
            rate_total = jnp.sum(rate_now)
            new_gate = renormed(gate_now[head_at], grad_gate, rate_total)
            new_up = renormed(up_now[head_at], grad_up, rate_total)
            new_down = renormed(down_now[head_at], grad_down, rate_total)
            query_gate = jnp.dot(query_now, new_gate.astype(jnp.bfloat16).T, preferred_element_type=jnp.float32)
            query_up = jnp.dot(query_now, new_up.astype(jnp.bfloat16).T, preferred_element_type=jnp.float32)
            query_hidden = (jax.nn.silu(query_gate) * query_up).astype(jnp.bfloat16)
            fast_out = jnp.dot(query_hidden, new_down.astype(jnp.bfloat16).T, preferred_element_type=jnp.float32)
            fast_out = fast_out / row_scale(fast_out)
            head_list.append((fast_out + attention[block_at, :, head_at, :]).astype(jnp.bfloat16))
            gate_list.append(new_gate)
            up_list.append(new_up)
            down_list.append(new_down)
        gate_now = jnp.stack(gate_list)
        up_now = jnp.stack(up_list)
        down_now = jnp.stack(down_list)
        outputs.append(jnp.concatenate(head_list, axis=1))
    joined = jnp.stack(outputs).reshape(BLOCKS * BLOCK, HEADS * DH)
    mixed_out = jnp.dot(joined, out_weight, preferred_element_type=jnp.float32).astype(jnp.bfloat16)
    return mixed_out.reshape(BLOCKS, BLOCK, D)
```

```python
import functools
import math

import jax
import jax.numpy as jnp
from jax import lax
from jax.experimental import pallas as pl
from jax.experimental.pallas import tpu as pltpu
from jax.sharding import PartitionSpec as P

DH = 384
WINDOW = 384
EPSILON = 1e-06
ROW_UNIT = 16
MESH = pl.DeviceIdType.MESH
NT = (((1,), (1,)), ((), ()))
NN = (((1,), (0,)), ((), ()))
TT = (((0,), (1,)), ((), ()))


def dot(a, b, dims):
    return lax.dot_general(a, b, dims, preferred_element_type=jnp.float32)


def sigmoid(x):
    return 0.5 * jnp.tanh(0.5 * x) + 0.5


def plan(bits, rows):
    orders = []
    for w in range(3):
        first = w % bits if bits else 0
        orders.append([first] + [j for j in range(bits) if j != first] if bits else [])
    sizes = [rows]
    for _ in range(bits):
        half = sizes[-1] // 2
        if sizes[-1] % 2 == 0 and half % ROW_UNIT == 0:
            sizes.append(half)
        else:
            break
    return orders, sizes


def kernel(
    bits, orders, sizes,
    q_ref, k_ref, v_ref, r_ref, g_ref, u_ref, d_ref, ow_ref,
    out_ref,
    halo_k, halo_v, att, wb, wf, grad, sb, rb, rate_sum, rate_in, ho, ho_peer, wo, wo_peer,
    rs_send, rs_recv, ag_send, ag_recv, halo_send, halo_recv, rate_send, rate_recv,
    ho_send, ho_recv, wo_send, wo_recv, local_sem,
):
    blocks, rows, width = q_ref.shape
    heads = width // DH
    tiles = rows // WINDOW
    count = lax.axis_size("tok")
    me = lax.axis_index("tok")
    core = lax.axis_index("head")
    peer = 1 - core
    nxt = lax.rem(me + 1, count)
    prv = lax.rem(me + count - 1, count)
    halvings = len(sizes) - 1
    cols = out_ref.shape[2]
    scale = 1.0 / math.sqrt(DH)

    bit = [lax.rem(lax.div(me, 2**j), 2) for j in range(bits)]
    partner = [me + (1 - 2 * bit[j]) * (2**j) for j in range(bits)]

    barrier = pltpu.get_barrier_semaphore()
    for j in range(bits):
        pl.semaphore_signal(barrier, inc=1, device_id={"tok": partner[j]}, device_id_type=MESH)
    pl.semaphore_signal(barrier, inc=1, device_id={"tok": nxt}, device_id_type=MESH)
    pl.semaphore_signal(barrier, inc=1, device_id={"tok": prv}, device_id_type=MESH)
    pl.semaphore_signal(barrier, inc=1, device_id={"head": peer}, device_id_type=MESH)
    pl.semaphore_wait(barrier, bits + 3)

    sent = []

    def remote(src, dst, ssem, rsem, device):
        return pltpu.make_async_remote_copy(
            src_ref=src, dst_ref=dst, send_sem=ssem, recv_sem=rsem,
            device_id=device, device_id_type=MESH,
        )

    def start(copy):
        copy.start()
        sent.append(copy)
        return copy

    offs = []
    for w in range(3):
        off = [0]
        for s in range(halvings):
            off.append(off[-1] + bit[orders[w][s]] * sizes[s + 1])
        offs.append([pl.multiple_of(o, ROW_UNIT) if i else 0 for i, o in enumerate(off)])
    region = [sum(sizes[1 : s + 1]) for s in range(halvings)]
    own = sizes[-1]
    for s in range(halvings, bits):
        region.append((region[-1] + (sizes[halvings] if s == halvings else own)) if region else 0)
    step_rows = [sizes[s + 1] if s < halvings else own for s in range(bits)]

    is_last = (me == count - 1).astype(jnp.int32)

    def halo(b):
        slot = lax.rem(b + is_last, blocks)
        for at, (src, dst) in enumerate(((k_ref, halo_k), (v_ref, halo_v))):
            start(remote(
                src.at[b, pl.ds(rows - WINDOW, WINDOW)], dst.at[slot],
                halo_send.at[at, b], halo_recv.at[at, slot], {"tok": nxt},
            ))

    def halo_wait(b):
        for at, (src, dst) in enumerate(((k_ref, halo_k), (v_ref, halo_v))):
            remote(
                src.at[b, pl.ds(rows - WINDOW, WINDOW)], dst.at[b],
                halo_send.at[at, b], halo_recv.at[at, b], {"tok": nxt},
            ).wait_recv()

    wo_local = pltpu.make_async_copy(
        ow_ref.at[:, pl.ds(pl.multiple_of(core * cols, 128), cols)], wo, local_sem
    )
    wo_local.start()
    wo_copy = start(remote(
        ow_ref.at[:, pl.ds(pl.multiple_of(peer * cols, 128), cols)], wo_peer,
        wo_send, wo_recv, {"head": peer},
    ))

    rate_sum[0] = jnp.zeros(rate_sum.shape[1:], jnp.float32)
    for h in range(heads):
        for b in range(blocks):
            total = jnp.sum(r_ref[h, b : b + 1, :], axis=1, keepdims=True)
            rate_sum[0, h * blocks + b : h * blocks + b + 1, :] = jnp.broadcast_to(total, (1, 128))

    def rate_copy(s):
        return remote(
            rate_sum.at[s], rate_in.at[s], rate_send.at[s], rate_recv.at[s], {"tok": partner[s]}
        )

    def rate_step(s):
        rate_copy(s).wait_recv()
        rate_sum[s + 1] = rate_sum[s] + rate_in[s]
        if s + 1 < bits:
            start(rate_copy(s + 1))

    def gradient(b, h):
        at = h * DH
        lanes = slice(at, at + DH)
        gate, up, down = wb[b, 3 * h], wb[b, 3 * h + 1], wb[b, 3 * h + 2]
        down_t = None
        for t in range(tiles):
            span = slice(t * WINDOW, (t + 1) * WINDOW)
            key = k_ref[b, span, lanes]
            value = v_ref[b, span, lanes]
            rate = r_ref[h, b : b + 1, span]
            h1 = dot(gate, key, NT)
            h3 = dot(up, key, NT)
            back = dot(down, value, TT) * rate
            sig = sigmoid(h1)
            active = h1 * sig
            hidden = (active * h3 * rate).astype(jnp.bfloat16)
            d3 = (back * active).astype(jnp.bfloat16)
            d1 = (back * h3 * (sig * (1.0 + h1 * (1.0 - sig)))).astype(jnp.bfloat16)
            t1, t3, t2 = dot(d1, key, NN), dot(d3, key, NN), dot(hidden, value, NN)
            if t == 0:
                grad[3 * h] = t1
                grad[3 * h + 1] = t3
                down_t = t2
            else:
                grad[3 * h] += t1
                grad[3 * h + 1] += t3
                down_t = down_t + t2
        grad[3 * h + 2] = down_t.T

    def rs_copy(b, h, w, s):
        i = 3 * h + w
        part = pl.ds(region[s], step_rows[s])
        return remote(
            sb.at[b, i, part], rb.at[b, i, part],
            rs_send.at[b, i, s], rs_recv.at[b, i, s], {"tok": partner[orders[w][s]]},
        )

    def rs_start(b, h, s):
        for w in range(3):
            i = 3 * h + w
            off = offs[w][min(s, halvings)]
            if s < halvings:
                off = off + (1 - bit[orders[w][s]]) * sizes[s + 1]
                off = pl.multiple_of(off, ROW_UNIT)
            piece = grad[i, pl.ds(off, step_rows[s]), :]
            sb[b, i, region[s] : region[s] + step_rows[s], :] = piece.astype(jnp.bfloat16)
            start(rs_copy(b, h, w, s))

    def rs_finish(b, h, s):
        for w in range(3):
            i = 3 * h + w
            rs_copy(b, h, w, s).wait_recv()
            got = rb[b, i, region[s] : region[s] + step_rows[s], :].astype(jnp.float32)
            keep = pl.ds(offs[w][min(s + 1, halvings)], step_rows[s])
            if s < halvings:
                grad[i, keep, :] = grad[i, keep, :] + got
            else:
                mine = sb[b, i, region[s] : region[s] + step_rows[s], :].astype(jnp.float32)
                grad[i, keep, :] = mine + got

    def row_mean(m):
        return jnp.mean(m * m, axis=1, keepdims=True) + EPSILON

    def update(b, h):
        row = h * blocks + b
        rate = rate_sum[bits, row : row + 1, 0:1]
        for w in range(3):
            i = 3 * h + w
            keep = pl.ds(offs[w][halvings], own)
            old = wf[i]
            new = old + grad[i, keep, :] / rate
            new = new * (jnp.sqrt(row_mean(old)) / jnp.sqrt(row_mean(new)))
            wf[i] = new
            wb[b + 1, i, keep, :] = new.astype(jnp.bfloat16)

    def ag_copy(b, h, w, s):
        i = 3 * h + w
        part = pl.ds(offs[w][s + 1], sizes[s + 1])
        return remote(
            wb.at[b + 1, i, part], wb.at[b + 1, i, part],
            ag_send.at[b, i, s], ag_recv.at[b, i, s], {"tok": partner[orders[w][s]]},
        )

    def ag_start(b, h, s):
        for w in range(3):
            start(ag_copy(b, h, w, s))

    def ag_finish(b, h, s):
        for w in range(3):
            ag_copy(b, h, w, s).wait_recv()

    row_at = lax.broadcasted_iota(jnp.int32, (WINDOW, WINDOW), 0)
    col_at = lax.broadcasted_iota(jnp.int32, (WINDOW, WINDOW), 1)

    def attend(b, h, t):
        lanes = slice(h * DH, (h + 1) * DH)
        span = slice(t * WINDOW, (t + 1) * WINDOW)
        query = q_ref[b, span, lanes]
        now = dot(query, k_ref[b, span, lanes], NT)
        if t == 0:
            before_k, before_v = halo_k[b, :, lanes], halo_v[b, :, lanes]
        else:
            earlier = slice((t - 1) * WINDOW, t * WINDOW)
            before_k, before_v = k_ref[b, earlier, lanes], v_ref[b, earlier, lanes]
        before = dot(query, before_k, NT)
        if t == 0 and b == 0:
            before = jnp.where(me == 0, -jnp.inf, before)
        here = col_at <= row_at
        scores = jnp.where(here, now, before) * scale
        expos = jnp.exp(scores - jnp.max(scores, axis=1, keepdims=True))
        probs = expos * (1.0 / jnp.sum(expos, axis=1, keepdims=True))
        near = jnp.where(here, probs, 0.0).astype(jnp.bfloat16)
        far = jnp.where(here, 0.0, probs).astype(jnp.bfloat16)
        att[b, span, lanes] = dot(near, v_ref[b, span, lanes], NN) + dot(far, before_v, NN)

    def ho_copy(b, h):
        part = (b, slice(None), pl.ds(h * DH, DH))
        return remote(
            ho.at[part], ho_peer.at[part], ho_send.at[b, h], ho_recv.at[b, h], {"head": peer}
        )

    def read_fast(b, h, t):
        lanes = slice(h * DH, (h + 1) * DH)
        span = slice(t * WINDOW, (t + 1) * WINDOW)
        query = q_ref[b, span, lanes]
        qg = dot(query, wb[b + 1, 3 * h], NT)
        qu = dot(query, wb[b + 1, 3 * h + 1], NT)
        hidden = (qg * sigmoid(qg) * qu).astype(jnp.bfloat16)
        fast = dot(hidden, wb[b + 1, 3 * h + 2], NT)
        fast = fast / jnp.sqrt(row_mean(fast))
        ho[b, span, lanes] = (fast + att[b, span, lanes]).astype(jnp.bfloat16)
        if t == tiles - 1:
            start(ho_copy(b, h))

    def project(b, t):
        span = slice(t * WINDOW, (t + 1) * WINDOW)
        total = dot(ho[b, span, :], wo[...], NN) + dot(ho_peer[b, span, :], wo_peer[...], NN)
        out_ref[b, span, :] = total.astype(jnp.bfloat16)

    halo(0)
    if bits:
        start(rate_copy(0))
    for h in range(heads):
        for w, init in enumerate((g_ref, u_ref, d_ref)):
            wb[0, 3 * h + w] = init[h].astype(jnp.bfloat16)
            wf[3 * h + w] = init[h, pl.ds(offs[w][halvings], own), :]

    part = functools.partial
    waiting = []
    for b in range(blocks):
        for t in range(1, tiles):
            for h in range(heads):
                waiting.append(part(attend, b, h, t))
    first_ready = len(waiting)
    del first_ready

    def halo_tiles(b):
        todo = [part(halo_wait, b)]
        todo += [part(attend, b, h, 0) for h in range(heads)]
        return todo

    def run(todo):
        if todo:
            todo.pop(0)()

    todo = list(waiting) + halo_tiles(0)
    for h in range(heads):
        gradient(0, h)
        rs_start(0, h, 0)
    for b in range(1, blocks):
        halo(b)
    for b in range(blocks):
        for s in range(bits):
            for h in range(heads):
                run(todo)
                rs_finish(b, h, s)
                if s + 1 < bits:
                    rs_start(b, h, s + 1)
            if b == 0:
                rate_step(s)
        for s in reversed(range(halvings)):
            for h in range(heads):
                if s == halvings - 1:
                    update(b, h)
                else:
                    ag_finish(b, h, s + 1)
                ag_start(b, h, s)
                run(todo)
        while todo:
            run(todo)
        for h in range(heads):
            if halvings:
                ag_finish(b, h, 0)
            if b + 1 < blocks:
                gradient(b + 1, h)
                rs_start(b + 1, h, 0)
        if b + 1 < blocks:
            todo = []
            for h in range(heads):
                todo += [part(read_fast, b, h, t) for t in range(tiles)]
            todo += halo_tiles(b + 1)
            if b == 0:
                todo.append(wo_local.wait)
                todo.append(wo_copy.wait_recv)
            todo += [ho_copy(b, h).wait_recv for h in range(heads)]
            todo += [part(project, b, t) for t in range(tiles)]
    last = blocks - 1
    if blocks == 1:
        wo_local.wait()
        wo_copy.wait_recv()
    for h in range(heads):
        for t in range(tiles):
            read_fast(last, h, t)
    for h in range(heads):
        ho_copy(last, h).wait_recv()
    for t in range(tiles):
        project(last, t)
    for copy in sent:
        copy.wait_send()


def shards(queries, key_rows, value_rows, step_rates, gate_init, up_init, down_init, out_weight):
    blocks, rows, width = queries.shape
    heads = width // DH
    count = lax.axis_size("tok")
    bits = count.bit_length() - 1
    cols = out_weight.shape[1] // lax.axis_size("head")
    orders, sizes = plan(bits, DH)
    halvings = len(sizes) - 1
    own = sizes[-1]
    staged = sum(sizes[1:]) + own * (bits - halvings)
    streams = 3 * heads
    bf16, f32 = jnp.bfloat16, jnp.float32
    dma = pltpu.SemaphoreType.DMA
    scratch = [
        pltpu.VMEM((blocks, WINDOW, width), bf16),
        pltpu.VMEM((blocks, WINDOW, width), bf16),
        pltpu.VMEM((blocks, rows, width), f32),
        pltpu.VMEM((blocks + 1, streams, DH, DH), bf16),
        pltpu.VMEM((streams, own, DH), f32),
        pltpu.VMEM((streams, DH, DH), f32),
        pltpu.VMEM((blocks, streams, staged, DH), bf16),
        pltpu.VMEM((blocks, streams, staged, DH), bf16),
        pltpu.VMEM((bits + 1, 8 * (-(-heads * blocks // 8)), 128), f32),
        pltpu.VMEM((bits, 8 * (-(-heads * blocks // 8)), 128), f32),
        pltpu.VMEM((blocks, rows, width), bf16),
        pltpu.VMEM((blocks, rows, width), bf16),
        pltpu.VMEM((out_weight.shape[0], cols), bf16),
        pltpu.VMEM((out_weight.shape[0], cols), bf16),
        dma((blocks, streams, bits)),
        dma((blocks, streams, bits)),
        dma((blocks, streams, halvings)),
        dma((blocks, streams, halvings)),
        dma((2, blocks)),
        dma((2, blocks)),
        dma((bits,)),
        dma((bits,)),
        dma((blocks, heads)),
        dma((blocks, heads)),
        dma,
        dma,
        dma,
    ]
    return pl.pallas_call(
        functools.partial(kernel, bits, orders, sizes),
        out_shape=jax.ShapeDtypeStruct((blocks, rows, cols), bf16),
        in_specs=[pl.BlockSpec(memory_space=pltpu.VMEM)] * 8,
        out_specs=pl.BlockSpec(memory_space=pltpu.VMEM),
        scratch_shapes=scratch,
        compiler_params=pltpu.CompilerParams(
            collective_id=0, has_side_effects=True, vmem_limit_bytes=60 * 1024 * 1024
        ),
        name="ttt_layer",
    )(queries, key_rows, value_rows, step_rates, gate_init, up_init, down_init, out_weight)


def solution(mesh):
    in_specs = (
        P(None, "tok", "head"),
        P(None, "tok", "head"),
        P(None, "tok", "head"),
        P("head", None, "tok"),
        P("head", None, None),
        P("head", None, None),
        P("head", None, None),
        P("head", None),
    )
    out_specs = P(None, "tok", "head")
    return jax.shard_map(shards, mesh=mesh, in_specs=in_specs, out_specs=out_specs, check_vma=False)
```
